32 devices in a mesh: section: 4 (over y, x), row: 4 (over z), col: 2 (over core).
Axes of the slice: x: 2, y: 2, z: 4, core: 2. Of those that a mesh axis runs over, the one named last changes fastest.
Arguments:
- section_inputs: bfloat16 [4, 512, 2048], P('section', 'col', 'row'), may hold values from -6 to 6
- out_grad: bfloat16 [4, 512, 2048], P('section', 'col', 'row'), may hold values from -6 to 6
- saved_gate: bfloat16 [4, 512, 8192], P('section', 'row', 'col'), may hold values from -6 to 6
- saved_up: bfloat16 [4, 512, 8192], P('section', 'row', 'col'), may hold values from -6 to 6
- gate_weight: bfloat16 [4, 2048, 8192], P('section', 'row', 'col'), may hold values from -0.125 to 0.125
- up_weight: bfloat16 [4, 2048, 8192], P('section', 'row', 'col'), may hold values from -0.125 to 0.125
- down_weight: bfloat16 [4, 8192, 2048], P('section', 'col', 'row'), may hold values from -0.0625 to 0.0625
- momentum_gate: float32 [4, 2048, 8192], P('section', 'row', 'col'), may hold values from -6 to 6
- momentum_up: float32 [4, 2048, 8192], P('section', 'row', 'col'), may hold values from -6 to 6
- momentum_down: float32 [4, 8192, 2048], P('section', 'col', 'row'), may hold values from -6 to 6
- noise_gate: bfloat16 [4, 2048, 8192], P('section', 'row', 'col'), may hold values from -6 to 6
- noise_up: bfloat16 [4, 2048, 8192], P('section', 'row', 'col'), may hold values from -6 to 6
- noise_down: bfloat16 [4, 8192, 2048], P('section', 'col', 'row'), may hold values from -6 to 6
Outputs:
- prev_grads: bfloat16 [4, 512, 2048], P('section', 'col', 'row')
- new_gate: bfloat16 [4, 2048, 8192], P('section', 'row', 'col')
- new_up: bfloat16 [4, 2048, 8192], P('section', 'row', 'col')
- new_down: bfloat16 [4, 8192, 2048], P('section', 'col', 'row')
- next_momentum_gate: float32 [4, 2048, 8192], P('section', 'row', 'col')
- next_momentum_up: float32 [4, 2048, 8192], P('section', 'row', 'col')
- next_momentum_down: float32 [4, 8192, 2048], P('section', 'col', 'row')
The draws below stay inside these ranges and needn't reach their ends.
All inputs are finite; a program needn't handle non-finite values.
Results may differ from the reference program's by a relative error of at most 0.025.
Values may be sent and summed in bfloat16 or wider, within the bound.
No kernel may reach another device: no remote copies, remote signals or barrier semaphores. Data moves between devices by JAX's collectives and lax.ppermute only.
A program may use at most 192 MiB of HBM per device.

```python
import jax
import jax.numpy as jnp
from jax import lax

D = 2048
FF = 8192
SECTIONS = 4
TOKENS = 512
N_ROW = 4
N_COL = 2


def block_levels(stream_key, shape, split, smallest, high):
    loudness = 1.0
    for axis_at, parts in split:
        steps = jax.random.uniform(jax.random.fold_in(jax.random.fold_in(stream_key, 6), axis_at), (parts,), jnp.float32, smallest / len(split), high / len(split))
        loudness = loudness * jnp.repeat(jnp.exp(steps), shape[axis_at] // parts).reshape((-1,) + (1,) * (len(shape) - 1 - axis_at))
    return loudness


def centred(key, extent, scale, limit, shards=(), held_as=jnp.bfloat16):
    drawn = scale * jax.random.normal(key, extent, jnp.float32)
    if shards:
        drawn = drawn * block_levels(key, extent, shards, -0.22, 0.18)
    return jnp.clip(drawn, -limit, limit).astype(held_as)


def setup_inputs(seed: int = 0) -> dict:
    splits = jax.random.split(jax.random.key(seed), 14)
    section_inputs = centred(splits[0], (SECTIONS, TOKENS, D), 1.0, 6.0, ((0, 4), (1, 2), (2, 4)))
    out_grad = centred(splits[1], (SECTIONS, TOKENS, D), 1.0, 6.0, ((0, 4), (1, 2), (2, 4)))
    saved_gate = centred(splits[2], (SECTIONS, TOKENS, FF), 1.0, 6.0, ((0, 4), (1, 4), (2, 2)))
    saved_up = centred(splits[3], (SECTIONS, TOKENS, FF), 1.0, 6.0, ((0, 4), (1, 4), (2, 2)))
    gate_weight = centred(splits[4], (SECTIONS, D, FF), D ** -0.5, 0.125, ((0, 4), (1, 4), (2, 2)))
    up_weight = centred(splits[5], (SECTIONS, D, FF), D ** -0.5, 0.125, ((0, 4), (1, 4), (2, 2)))
    down_weight = centred(splits[6], (SECTIONS, FF, D), FF ** -0.5, 0.0625, ((0, 4), (1, 2), (2, 4)))
    momentum_gate = centred(splits[7], (SECTIONS, D, FF), 1.0, 6.0, ((0, 4), (1, 4), (2, 2)), jnp.float32)
    momentum_up = centred(splits[8], (SECTIONS, D, FF), 1.0, 6.0, ((0, 4), (1, 4), (2, 2)), jnp.float32)
    momentum_down = centred(splits[9], (SECTIONS, FF, D), 1.0, 6.0, ((0, 4), (1, 2), (2, 4)), jnp.float32)
    noise_gate = centred(splits[10], (SECTIONS, D, FF), 1.0, 6.0, ((0, 4), (1, 4), (2, 2)))
    noise_up = centred(splits[11], (SECTIONS, D, FF), 1.0, 6.0, ((0, 4), (1, 4), (2, 2)))
    noise_down = centred(splits[12], (SECTIONS, FF, D), 1.0, 6.0, ((0, 4), (1, 2), (2, 4)))
    return dict(section_inputs=section_inputs, out_grad=out_grad, saved_gate=saved_gate, saved_up=saved_up, gate_weight=gate_weight, up_weight=up_weight, down_weight=down_weight, momentum_gate=momentum_gate, momentum_up=momentum_up, momentum_down=momentum_down, noise_gate=noise_gate, noise_up=noise_up, noise_down=noise_down)


FRICTION = 0.1
DRIFT = 0.01


def blockwise_sum(pairs, blocks):
    width = pairs[0][0].shape[1] // blocks
    total = jnp.zeros((pairs[0][0].shape[0], pairs[0][1].shape[1]), jnp.float32)
    for block in range(blocks):
        partial_value = jnp.zeros_like(total)
        for left, right in pairs:
            left_block = left[:, block * width:(block + 1) * width]
            right_block = right[block * width:(block + 1) * width, :]
            partial_value = partial_value + jnp.dot(left_block, right_block, preferred_element_type=jnp.float32)
        rounded = lax.optimization_barrier(partial_value.astype(jnp.bfloat16))
        total = total + rounded.astype(jnp.float32)
    return total


def pre_grads(hidden_grad, gate_pre, up_pre):
    gate_wide = gate_pre.astype(jnp.float32)
    up_wide = up_pre.astype(jnp.float32)
    sigmoid_gate = jax.nn.sigmoid(gate_wide)
    silu_gate = gate_wide * sigmoid_gate
    slope = sigmoid_gate * (1.0 + gate_wide * (1.0 - sigmoid_gate))
    gate_grad = (hidden_grad * up_wide * slope).astype(jnp.bfloat16)
    up_grad = (hidden_grad * silu_gate).astype(jnp.bfloat16)
    hidden_saved = (silu_gate * up_wide).astype(jnp.bfloat16)
    return hidden_saved, gate_grad, up_grad


def sghmc_step(weight, momentum, gradient, noise, kick_scale):
    moved = (1.0 - FRICTION) * momentum - kick_scale * gradient + (2.0 * FRICTION) ** 0.5 * noise.astype(jnp.float32)
    fresh = (weight.astype(jnp.float32) + DRIFT * moved).astype(jnp.bfloat16)
    return fresh, moved


def reference(section_inputs, out_grad, saved_gate, saved_up, gate_weight, up_weight, down_weight, momentum_gate, momentum_up, momentum_down, noise_gate, noise_up, noise_down):
    kick_scale = float(TOKENS) ** -0.5
    input_grads = []
    gates, ups, downs, gate_moms, up_moms, down_moms = [], [], [], [], [], []
    for section in range(SECTIONS):
        inputs_now = section_inputs[section]
        grads_now = out_grad[section]
        hidden_grad = blockwise_sum([(grads_now, down_weight[section].T)], N_ROW)
        hidden_saved, gate_grad, up_grad = pre_grads(hidden_grad, saved_gate[section], saved_up[section])
        down_wgrad = jnp.dot(hidden_saved.T, grads_now, preferred_element_type=jnp.float32)
        gate_wgrad = jnp.dot(inputs_now.T, gate_grad, preferred_element_type=jnp.float32)
        up_wgrad = jnp.dot(inputs_now.T, up_grad, preferred_element_type=jnp.float32)
        input_grad = blockwise_sum([(gate_grad, gate_weight[section].T), (up_grad, up_weight[section].T)], N_COL).astype(jnp.bfloat16)
        input_grads.append(input_grad)
        fresh, moved = sghmc_step(gate_weight[section], momentum_gate[section], gate_wgrad, noise_gate[section], kick_scale)
        gates.append(fresh)
        gate_moms.append(moved)
        fresh, moved = sghmc_step(up_weight[section], momentum_up[section], up_wgrad, noise_up[section], kick_scale)
        ups.append(fresh)
        up_moms.append(moved)
        fresh, moved = sghmc_step(down_weight[section], momentum_down[section], down_wgrad, noise_down[section], kick_scale)
        downs.append(fresh)
        down_moms.append(moved)
    stacked = jnp.stack(input_grads)
    prev_grads = jnp.concatenate([stacked[1:], jnp.zeros_like(stacked[:1])], axis=0)
    return (prev_grads, jnp.stack(gates), jnp.stack(ups), jnp.stack(downs), jnp.stack(gate_moms), jnp.stack(up_moms), jnp.stack(down_moms))
```

```python
import functools

import jax
import jax.numpy as jnp
from jax import lax
from jax.experimental import pallas as pl
from jax.experimental.pallas import tpu as pltpu
from jax.sharding import PartitionSpec as P

FRICTION = 0.1
DRIFT = 0.01
CHUNKS = (2, 2, 2, 1, 1)
VMEM_LIMIT = 56 * 1024 * 1024


def from_behind(shard, axis, by):
    size = lax.axis_size(axis)
    pairs = [(i, i + by) for i in range(size) if 0 <= i + by < size]
    return lax.ppermute(shard, axis, pairs)


def contract(left, right, left_dim, right_dim):
    return lax.dot_general(
        left, right, (((left_dim,), (right_dim,)), ((), ())), preferred_element_type=jnp.float32
    )


def moved_and_fresh(weight, momentum, gradient, noise, kick_scale):
    moved = (
        (1.0 - FRICTION) * momentum
        - kick_scale * gradient
        + (2.0 * FRICTION) ** 0.5 * noise.astype(jnp.float32)
    )
    fresh = (weight.astype(jnp.float32) + DRIFT * moved).astype(jnp.bfloat16)
    return moved, fresh


def add_kernel(left, right, *rest):
    total = rest[-1]
    rows = min(128, left.shape[0])

    @pl.loop(0, left.shape[0] // rows)
    def _(step):
        at = pl.ds(pl.multiple_of(step * rows, rows), rows)
        total[at, :] = left[at, :] + right[at, :]


def add_wide(left, right, ties=()):
    return pl.pallas_call(
        add_kernel,
        in_specs=[pl.BlockSpec(memory_space=pltpu.VMEM)] * 2
        + [pl.BlockSpec(memory_space=pl.ANY)] * len(ties),
        out_specs=pl.BlockSpec(memory_space=pltpu.VMEM),
        out_shape=jax.ShapeDtypeStruct(left.shape, jnp.bfloat16),
        cost_estimate=pl.CostEstimate(
            flops=left.size, bytes_accessed=6 * left.size, transcendentals=0
        ),
        name="add_wide",
    )(left, right, *ties)


def same_kernel(*refs):
    del refs


def after(value, *ties):
    anywhere = pl.BlockSpec(memory_space=pl.ANY)
    return pl.pallas_call(
        same_kernel,
        in_specs=[anywhere] * (1 + len(ties)),
        out_specs=anywhere,
        out_shape=jax.ShapeDtypeStruct(value.shape, value.dtype),
        input_output_aliases={0: 0},
        cost_estimate=pl.CostEstimate(flops=0, bytes_accessed=0, transcendentals=0),
        name="after",
    )(value, *ties)


def tile_of(width, largest=512):
    for tile in (largest, 256, 128):
        if width % tile == 0:
            return tile
    return width


def pre_grads(flag, received, held, gate_factor, up_factor):
    hidden_grad = jnp.where(
        flag[0] == 1, received[...].astype(jnp.float32), held[...].astype(jnp.float32)
    )
    gate_grad = (hidden_grad * gate_factor[...].astype(jnp.float32)).astype(jnp.bfloat16)
    up_grad = (hidden_grad * up_factor[...].astype(jnp.float32)).astype(jnp.bfloat16)
    return gate_grad, up_grad


def update_kernel(
    kick_scale,
    with_part,
    first,
    flag,
    received,
    held,
    gate_factor,
    up_factor,
    inputs_t,
    gate_weight,
    up_weight,
    momentum_gate,
    momentum_up,
    noise_gate,
    noise_up,
    *rest,
):
    if with_part:
        part = rest[-1]
        rest = rest[:-1]

        @pl.when(pl.program_id(0) == 0)
        def _():
            part[...] = jnp.zeros_like(part) if first else rest[0][...]

    new_gate, new_up, next_gate, next_up = rest[-4:]
    gate_grad, up_grad = pre_grads(flag, received, held, gate_factor, up_factor)
    gate_here = gate_weight[...]
    up_here = up_weight[...]
    if with_part:
        part[...] += contract(gate_grad, gate_here, 1, 1) + contract(up_grad, up_here, 1, 1)
    gate_wgrad = contract(inputs_t[...], gate_grad, 1, 0)
    moved, fresh = moved_and_fresh(
        gate_here, momentum_gate[...], gate_wgrad, noise_gate[...], kick_scale
    )
    next_gate[...] = moved
    new_gate[...] = fresh
    up_wgrad = contract(inputs_t[...], up_grad, 1, 0)
    moved, fresh = moved_and_fresh(up_here, momentum_up[...], up_wgrad, noise_up[...], kick_scale)
    next_up[...] = moved
    new_up[...] = fresh


def chunk_specs(start, tokens, rows, width, tile):
    steps = width // tile
    at = start // tile
    here = pl.BlockSpec((tokens, tile), lambda j: (0, j))
    there = pl.BlockSpec((tokens, tile), lambda j: (0, at + j))
    block = pl.BlockSpec((rows, tile), lambda j: (0, at + j))
    flag = pl.BlockSpec(memory_space=pltpu.SMEM)
    return steps, block, [flag, here, here, there, there]


def part_kernel(
    halves, col, flag, received, held, gate_factor, up_factor, gate_weight, up_weight, before, *rest
):
    outs, part = rest[:-1], rest[-1]

    @pl.when(pl.program_id(0) == 0)
    def _():
        part[...] = before[...]

    gate_grad, up_grad = pre_grads(flag, received, held, gate_factor, up_factor)
    part[...] += contract(gate_grad, gate_weight[...], 1, 1) + contract(
        up_grad, up_weight[...], 1, 1
    )

    @pl.when(pl.program_id(0) == pl.num_programs(0) - 1)
    def _():
        if not halves:
            outs[0][...] = part[...].astype(jnp.bfloat16)
            return
        half = part.shape[0] // 2
        for out, which in ((outs[0], col[0]), (outs[1], 1 - col[0])):
            at = pl.ds(pl.multiple_of(which * half, half), half)
            out[...] = part[at, :].astype(jnp.bfloat16)


def part_step(start, hidden, factors, weights, part, axis):
    received, held, flag = hidden
    tokens, width = held.shape
    rows = weights[0].shape[0]
    halves = lax.axis_size(axis) == 2
    tile = tile_of(width)
    steps, block, in_specs = chunk_specs(start, tokens, rows, width, tile)
    whole = pl.BlockSpec((tokens, rows), lambda j: (0, 0))
    half = pl.BlockSpec((tokens // 2, rows), lambda j: (0, 0))
    index = lax.axis_index(axis).astype(jnp.int32).reshape((1,))
    return pl.pallas_call(
        functools.partial(part_kernel, halves),
        grid=(steps,),
        in_specs=[pl.BlockSpec(memory_space=pltpu.SMEM)] + in_specs + [block] * 2 + [whole],
        out_specs=[half] * 2 if halves else [whole],
        out_shape=[jax.ShapeDtypeStruct((tokens // 2, rows), jnp.bfloat16)] * 2
        if halves
        else [jax.ShapeDtypeStruct((tokens, rows), jnp.bfloat16)],
        scratch_shapes=[pltpu.VMEM((tokens, rows), jnp.float32)],
        compiler_params=pltpu.CompilerParams(vmem_limit_bytes=VMEM_LIMIT),
        cost_estimate=pl.CostEstimate(
            flops=4 * tokens * rows * width,
            bytes_accessed=(8 * tokens + 4 * rows) * width + 6 * tokens * rows,
            transcendentals=0,
        ),
        name="part_step",
    )(index, flag, received, held, *factors, *weights, part)


def update_step(kick_scale, start, hidden, factors, inputs_t, arrays, part, made, with_part):
    received, held, flag = hidden
    tokens, width = held.shape
    rows, columns = arrays[0].shape
    tile = tile_of(width, 512 if with_part else 256)
    first = part is None
    steps, block, in_specs = chunk_specs(start, tokens, rows, width, tile)
    whole_inputs = pl.BlockSpec((rows, tokens), lambda j: (0, 0))
    whole_part = pl.BlockSpec((tokens, rows), lambda j: (0, 0))
    in_specs += [whole_inputs] + [block] * 6
    operands = [flag, received, held, *factors, inputs_t, *arrays]
    if with_part and not first:
        in_specs.append(whole_part)
        operands.append(part)
    aliases = {}
    if made is not None:
        aliases = {len(operands) + i: i for i in range(4)}
        in_specs += [pl.BlockSpec(memory_space=pl.ANY)] * 4
        operands += made
    shape = (rows, columns)
    out_specs = [block] * 4
    out_shape = [
        jax.ShapeDtypeStruct(shape, jnp.bfloat16),
        jax.ShapeDtypeStruct(shape, jnp.bfloat16),
        jax.ShapeDtypeStruct(shape, jnp.float32),
        jax.ShapeDtypeStruct(shape, jnp.float32),
    ]
    if with_part:
        out_specs.append(whole_part)
        out_shape.append(jax.ShapeDtypeStruct((tokens, rows), jnp.float32))
    outs = pl.pallas_call(
        functools.partial(update_kernel, kick_scale, with_part, first),
        grid=(steps,),
        in_specs=in_specs,
        out_specs=out_specs,
        out_shape=out_shape,
        input_output_aliases=aliases,
        compiler_params=pltpu.CompilerParams(vmem_limit_bytes=VMEM_LIMIT),
        cost_estimate=pl.CostEstimate(
            flops=(8 if with_part else 4) * tokens * rows * width,
            bytes_accessed=(8 * tokens + 28 * rows) * width,
            transcendentals=0,
        ),
        name="update_step",
    )(*operands)
    return (outs[4] if with_part else None), tuple(outs[:4])


def saved_kernel(kick_scale, size, table, *refs):
    gate_pieces = refs[: 2 * size - 1]
    up_pieces = refs[2 * size - 1 : 4 * size - 2]
    grads, weight, momentum, noise = refs[4 * size - 2 : 4 * size + 2]
    new_down, next_down, gate_factor, up_factor, hidden = refs[4 * size + 2 :]
    rows = gate_pieces[0].shape[0]

    def piece(pieces, at):
        if at == 0:
            return pieces[0][...].astype(jnp.float32)
        one, other = pieces[2 * at - 1], pieces[2 * at]
        return jnp.where(
            table[at] == 1, one[...].astype(jnp.float32), other[...].astype(jnp.float32)
        )

    for part in range(size):
        gate_wide = piece(gate_pieces, part)
        up_wide = piece(up_pieces, part)
        sigmoid_gate = 0.5 + 0.5 * jnp.tanh(0.5 * gate_wide)
        silu_gate = gate_wide * sigmoid_gate
        slope = sigmoid_gate * (1.0 + gate_wide * (1.0 - sigmoid_gate))
        at = pl.ds(pl.multiple_of(table[size + part] * rows, rows), rows)
        gate_factor[at, :] = (up_wide * slope).astype(jnp.bfloat16)
        up_factor[at, :] = silu_gate.astype(jnp.bfloat16)
        hidden[at, :] = (silu_gate * up_wide).astype(jnp.bfloat16)
    wgrad = contract(hidden[...], grads[...], 0, 0)
    moved, fresh = moved_and_fresh(weight[...], momentum[...], wgrad, noise[...], kick_scale)
    next_down[...] = moved
    new_down[...] = fresh


def saved_step(kick_scale, size, table, gate_pieces, up_pieces, grads, weight, momentum, noise):
    rows, width = gate_pieces[0][0].shape
    tokens, columns = grads.shape
    tile = tile_of(width)
    pieces = [*gate_pieces, *up_pieces]
    piece_specs = [pl.BlockSpec((rows, tile), lambda j, at=at: (at, j)) for _, at in pieces]
    block = pl.BlockSpec((tile, columns), lambda j: (j, 0))
    whole = pl.BlockSpec((tokens, columns), lambda j: (0, 0))
    factor = pl.BlockSpec((tokens, tile), lambda j: (0, j))
    return pl.pallas_call(
        functools.partial(saved_kernel, kick_scale, size),
        grid=(width // tile,),
        in_specs=[pl.BlockSpec(memory_space=pltpu.SMEM)]
        + piece_specs
        + [whole]
        + [block] * 3,
        out_specs=[block, block, factor, factor],
        out_shape=[
            jax.ShapeDtypeStruct(weight.shape, jnp.bfloat16),
            jax.ShapeDtypeStruct(weight.shape, jnp.float32),
            jax.ShapeDtypeStruct((tokens, width), jnp.bfloat16),
            jax.ShapeDtypeStruct((tokens, width), jnp.bfloat16),
        ],
        scratch_shapes=[pltpu.VMEM((tokens, tile), jnp.bfloat16)],
        compiler_params=pltpu.CompilerParams(vmem_limit_bytes=VMEM_LIMIT),
        cost_estimate=pl.CostEstimate(
            flops=2 * tokens * width * columns,
            bytes_accessed=12 * tokens * width + 14 * width * columns,
            transcendentals=tokens * width,
        ),
        name="saved_step",
    )(table, *[array for array, _ in pieces], grads, weight, momentum, noise)


def relay_step(behind, ahead, axis, step):
    size = lax.axis_size(axis)
    up = [(i, i + 1) for i in range(step - 1, size - 1)]
    down = [(i, i - 1) for i in range(1, size - step + 1)]
    return lax.ppermute(behind, axis, up), lax.ppermute(ahead, axis, down)


def relayed(arrays, axis):
    size = lax.axis_size(axis)
    me = lax.axis_index(axis).astype(jnp.int32)
    pieces = []
    for own in arrays:
        behind, ahead = [own], [own]
        for step in range(1, size):
            from_back, from_front = relay_step(behind[-1], ahead[-1], axis, step)
            behind.append(from_back)
            ahead.append(from_front)
        pieces.append([(own, 0)])
        for back in range(1, size):
            pieces[-1] += [(behind[back], 0), (ahead[size - back], 0)]
    backs = jnp.arange(size, dtype=jnp.int32)
    table = jnp.concatenate([(me >= backs).astype(jnp.int32), (me - backs + size) % size])
    return pieces, table


OUTWARD = ((1, 0), (2, 3))
INWARD = ((0, 1), (3, 2))
MIDDLE = ((1, 2), (2, 1))


def relayed_by_four(arrays, terms, axis):
    me = lax.axis_index(axis).astype(jnp.int32)
    gate, up = arrays
    gate_b1, gate_a1 = relay_step(gate, gate, axis, 1)
    up_b1, up_a1 = relay_step(up, up, axis, 1)
    gate_b2, gate_a2 = relay_step(gate_b1, gate_a1, axis, 2)
    up_b2, up_a2 = relay_step(up_b1, up_a1, axis, 2)
    gate_out3 = lax.ppermute(jnp.where(me == 1, gate_a2, gate_b2), axis, OUTWARD)
    up_out3 = lax.ppermute(jnp.where(me == 1, up_a2, up_b2), axis, OUTWARD)
    terms, ins = list(terms), []
    for at in range(len(terms)):
        if at in (1, 2):
            terms[at] = after(terms[at], ins[-1])
        ins.append(lax.ppermute(terms[at], axis, INWARD))
    inner, mids = [], []
    sums = []

    def send_inner(at, *ties):
        inner.append(add_wide(terms[at], ins[at], ties))
        mids.append(lax.ppermute(inner[at], axis, MIDDLE))

    def send_total(at, *ties):
        sums.append(outward_sum(add_wide(inner[at], mids[at], ties), axis))

    send_inner(0, up_a2, up_b2)
    send_inner(1, gate_out3)
    send_total(0, gate_out3)
    send_inner(2, mids[0])
    send_total(1, up_out3)
    send_inner(3, mids[1])
    send_inner(4, mids[2])
    pieces = [
        [(gate, 0), (gate_a1, 0), (gate_b1, 0), (gate_a2, 0), (gate_b2, 0)],
        [(up, 0), (up_a1, 0), (up_b1, 0), (up_a2, 0), (up_b2, 0)],
    ]
    pieces[0] += [(gate_out3, 0), (gate_b1, 0)]
    pieces[1] += [(up_out3, 0), (up_b1, 0)]
    end = (me == 0) | (me == 3)
    flags = [me < 3, me < 3, me < 2, end]
    places = [me, jnp.where(me < 3, me + 1, 2), (me + 2) % 4, jnp.where(end, 3 - me, me - 1)]
    table = jnp.stack([flag.astype(jnp.int32) for flag in flags] + places)
    return pieces, table, sums, send_total


def inward_sum(term, axis, ties):
    size = lax.axis_size(axis)
    held = term
    for step in range(size // 2 - 1):
        pairs = [(step, step + 1), (size - 1 - step, size - 2 - step)]
        held = add_wide(held, lax.ppermute(held, axis, pairs), ties if step == 0 else ())
    return held


def middle_sum(held, axis, ties):
    half = lax.axis_size(axis) // 2
    across = lax.ppermute(held, axis, [(half - 1, half), (half, half - 1)])
    return add_wide(held, across, ties), across


def outward_sum(held, axis):
    size = lax.axis_size(axis)
    index = lax.axis_index(axis)
    half = size // 2
    received, flag = held, jnp.zeros((1,), jnp.int32)
    for step in range(half - 1):
        if step:
            held = jnp.where(flag[0] == 1, received, held)
        pairs = [(half - 1 - step, half - 2 - step), (half + step, half + 1 + step)]
        received = lax.ppermute(held, axis, pairs)
        arrived = (index == half - 2 - step) | (index == half + 1 + step)
        flag = arrived.astype(jnp.int32).reshape((1,))
    return received, held, flag


def row_sums(terms, axis):
    sums = []
    for term in terms:
        if lax.axis_size(axis) % 2:
            total = lax.psum(term, axis)
            sums.append((total, total, jnp.zeros((1,), jnp.int32)))
        else:
            held, _ = middle_sum(inward_sum(term, axis, ()), axis, ())
            sums.append(outward_sum(held, axis))
    return sums


def parts_sum(parts, axis):
    if len(parts) == 1:
        return lax.psum_scatter(parts[0], axis, scatter_dimension=0, tiled=True)
    return add_wide(parts[0], lax.ppermute(parts[1], axis, [(0, 1), (1, 0)]))


def shards(
    section_inputs,
    out_grad,
    saved_gate,
    saved_up,
    gate_weight,
    up_weight,
    down_weight,
    momentum_gate,
    momentum_up,
    momentum_down,
    noise_gate,
    noise_up,
    noise_down,
):
    size = lax.axis_size("row")
    saved = (saved_gate[0], saved_up[0])
    grads_full = lax.all_gather(out_grad[0], "col", axis=0, tiled=True)
    inputs_full = lax.all_gather(section_inputs[0], "col", axis=0, tiled=True)
    inputs_t = inputs_full.T
    tokens = inputs_full.shape[0]
    kick_scale = float(tokens) ** (-0.5)
    down_local = down_weight[0]
    unit = down_local.shape[0] // sum(CHUNKS)
    starts = [unit * sum(CHUNKS[:at]) for at in range(len(CHUNKS))]
    stops = starts[1:] + [down_local.shape[0]]
    terms = [
        contract(grads_full, down_local[start:stop], 1, 1).astype(jnp.bfloat16)
        for start, stop in zip(starts, stops)
    ]
    send_total = None
    if size == 4:
        pieces, table, sums, send_total = relayed_by_four(saved, terms, "row")
    else:
        pieces, table = relayed(saved, "row")
        sums = row_sums(terms, "row")

    new_down, next_down, *factors = saved_step(
        kick_scale,
        size,
        table,
        *pieces,
        grads_full,
        down_local,
        momentum_down[0],
        noise_down[0],
    )
    weights = (gate_weight[0], up_weight[0])
    arrays = weights + (momentum_gate[0], momentum_up[0], noise_gate[0], noise_up[0])
    if send_total is not None:
        send_total(2, factors[0])
    part, made = None, None
    for at, start in enumerate(starts[:-1]):
        part, made = update_step(
            kick_scale, start, sums[at], factors, inputs_t, arrays, part, made, True
        )
        if at < 2 and send_total is not None:
            send_total(3 + at, part)
    parts = part_step(starts[-1], sums[-1], factors, weights, part, "col")
    _, made = update_step(
        kick_scale, starts[-1], sums[-1], factors, inputs_t, arrays, None, made, False
    )
    new_gate, new_up, next_gate, next_up = made
    input_grad = parts_sum(parts, "col")
    passed = from_behind(input_grad, "section", -1)
    return tuple(
        value[None]
        for value in (passed, new_gate, new_up, new_down, next_gate, next_up, next_down)
    )


def solution(mesh):
    in_specs = (
        P("section", "col", "row"),
        P("section", "col", "row"),
        P("section", "row", "col"),
        P("section", "row", "col"),
        P("section", "row", "col"),
        P("section", "row", "col"),
        P("section", "col", "row"),
        P("section", "row", "col"),
        P("section", "row", "col"),
        P("section", "col", "row"),
        P("section", "row", "col"),
        P("section", "row", "col"),
        P("section", "col", "row"),
    )
    out_specs = (
        P("section", "col", "row"),
        P("section", "row", "col"),
        P("section", "row", "col"),
        P("section", "col", "row"),
        P("section", "row", "col"),
        P("section", "row", "col"),
        P("section", "col", "row"),
    )
    return jax.shard_map(shards, mesh=mesh, in_specs=in_specs, out_specs=out_specs, check_vma=False)
```

```python
import functools

import jax
import jax.numpy as jnp
from jax import lax
from jax.experimental import pallas as pl
from jax.experimental.pallas import tpu as pltpu
from jax.sharding import PartitionSpec as P

FRICTION = 0.1
DRIFT = 0.01
CHUNKS = (2, 2, 2, 1, 1)
VMEM_LIMIT = 56 * 1024 * 1024


def from_behind(shard, axis, by):
    size = lax.axis_size(axis)
    pairs = [(i, i + by) for i in range(size) if 0 <= i + by < size]
    return lax.ppermute(shard, axis, pairs)


def contract(left, right, left_dim, right_dim):
    return lax.dot_general(
        left, right, (((left_dim,), (right_dim,)), ((), ())), preferred_element_type=jnp.float32
    )


def moved_and_fresh(weight, momentum, gradient, noise, kick_scale):
    moved = (
        (1.0 - FRICTION) * momentum
        - kick_scale * gradient
        + (2.0 * FRICTION) ** 0.5 * noise.astype(jnp.float32)
    )
    fresh = (weight.astype(jnp.float32) + DRIFT * moved).astype(jnp.bfloat16)
    return moved, fresh


def after(value, *ties):
    return lax.optimization_barrier((value, *ties))[0]


def add_wide(left, right, ties=()):
    right = after(right, *ties) if ties else right
    return (left.astype(jnp.float32) + right.astype(jnp.float32)).astype(jnp.bfloat16)


def tile_of(width, largest=512):
    for tile in (largest, 256, 128):
        if width % tile == 0:
            return tile
    return width


def pre_grads(flag, received, held, gate_factor, up_factor):
    hidden_grad = jnp.where(
        flag[0] == 1, received[...].astype(jnp.float32), held[...].astype(jnp.float32)
    )
    gate_grad = (hidden_grad * gate_factor[...].astype(jnp.float32)).astype(jnp.bfloat16)
    up_grad = (hidden_grad * up_factor[...].astype(jnp.float32)).astype(jnp.bfloat16)
    return gate_grad, up_grad


def update_kernel(
    kick_scale,
    with_part,
    first,
    flag,
    received,
    held,
    gate_factor,
    up_factor,
    inputs_t,
    gate_weight,
    up_weight,
    momentum_gate,
    momentum_up,
    noise_gate,
    noise_up,
    *rest,
):
    if with_part:
        part = rest[-1]
        rest = rest[:-1]

        @pl.when(pl.program_id(0) == 0)
        def _():
            part[...] = jnp.zeros_like(part) if first else rest[0][...]

    new_gate, new_up, next_gate, next_up = rest[-4:]
    gate_grad, up_grad = pre_grads(flag, received, held, gate_factor, up_factor)
    gate_here = gate_weight[...]
    up_here = up_weight[...]
    if with_part:
        part[...] += contract(gate_grad, gate_here, 1, 1) + contract(up_grad, up_here, 1, 1)
    gate_wgrad = contract(inputs_t[...], gate_grad, 1, 0)
    moved, fresh = moved_and_fresh(
        gate_here, momentum_gate[...], gate_wgrad, noise_gate[...], kick_scale
    )
    next_gate[...] = moved
    new_gate[...] = fresh
    up_wgrad = contract(inputs_t[...], up_grad, 1, 0)
    moved, fresh = moved_and_fresh(up_here, momentum_up[...], up_wgrad, noise_up[...], kick_scale)
    next_up[...] = moved
    new_up[...] = fresh


def chunk_specs(start, base, tokens, rows, width, tile):
    steps = width // tile
    at = start // tile
    there_at = (start - base) // tile
    here = pl.BlockSpec((tokens, tile), lambda j: (0, j))
    there = pl.BlockSpec((tokens, tile), lambda j: (0, there_at + j))
    block = pl.BlockSpec((rows, tile), lambda j: (0, at + j))
    flag = pl.BlockSpec(memory_space=pltpu.SMEM)
    return steps, block, [flag, here, here, there, there]


def part_kernel(
    halves, col, flag, received, held, gate_factor, up_factor, gate_weight, up_weight, before, *rest
):
    outs, part = rest[:-1], rest[-1]

    @pl.when(pl.program_id(0) == 0)
    def _():
        part[...] = before[...]

    gate_grad, up_grad = pre_grads(flag, received, held, gate_factor, up_factor)
    part[...] += contract(gate_grad, gate_weight[...], 1, 1) + contract(
        up_grad, up_weight[...], 1, 1
    )

    @pl.when(pl.program_id(0) == pl.num_programs(0) - 1)
    def _():
        if not halves:
            outs[0][...] = part[...].astype(jnp.bfloat16)
            return
        half = part.shape[0] // 2
        for out, which in ((outs[0], col[0]), (outs[1], 1 - col[0])):
            at = pl.ds(pl.multiple_of(which * half, half), half)
            out[...] = part[at, :].astype(jnp.bfloat16)


def part_step(start, hidden, factored, weights, part, axis):
    received, held, flag = hidden
    base, factors = factored
    tokens, width = held.shape
    rows = weights[0].shape[0]
    halves = lax.axis_size(axis) == 2
    tile = tile_of(width)
    steps, block, in_specs = chunk_specs(start, base, tokens, rows, width, tile)
    whole = pl.BlockSpec((tokens, rows), lambda j: (0, 0))
    half = pl.BlockSpec((tokens // 2, rows), lambda j: (0, 0))
    index = lax.axis_index(axis).astype(jnp.int32).reshape((1,))
    return pl.pallas_call(
        functools.partial(part_kernel, halves),
        grid=(steps,),
        in_specs=[pl.BlockSpec(memory_space=pltpu.SMEM)] + in_specs + [block] * 2 + [whole],
        out_specs=[half] * 2 if halves else [whole],
        out_shape=[jax.ShapeDtypeStruct((tokens // 2, rows), jnp.bfloat16)] * 2
        if halves
        else [jax.ShapeDtypeStruct((tokens, rows), jnp.bfloat16)],
        scratch_shapes=[pltpu.VMEM((tokens, rows), jnp.float32)],
        compiler_params=pltpu.CompilerParams(vmem_limit_bytes=VMEM_LIMIT),
        cost_estimate=pl.CostEstimate(
            flops=4 * tokens * rows * width,
            bytes_accessed=(8 * tokens + 4 * rows) * width + 6 * tokens * rows,
            transcendentals=0,
        ),
        name="part_step",
    )(index, flag, received, held, *factors, *weights, part)


def update_step(kick_scale, start, hidden, factored, inputs_t, arrays, part, made, with_part):
    received, held, flag = hidden
    base, factors = factored
    tokens, width = held.shape
    rows, columns = arrays[0].shape
    tile = tile_of(width, 512 if with_part else 256)
    first = part is None
    steps, block, in_specs = chunk_specs(start, base, tokens, rows, width, tile)
    whole_inputs = pl.BlockSpec((rows, tokens), lambda j: (0, 0))
    whole_part = pl.BlockSpec((tokens, rows), lambda j: (0, 0))
    in_specs += [whole_inputs] + [block] * 6
    operands = [flag, received, held, *factors, inputs_t, *arrays]
    if with_part and not first:
        in_specs.append(whole_part)
        operands.append(part)
    aliases = {}
    if made is not None:
        aliases = {len(operands) + i: i for i in range(4)}
        in_specs += [pl.BlockSpec(memory_space=pl.ANY)] * 4
        operands += made
    shape = (rows, columns)
    out_specs = [block] * 4
    out_shape = [
        jax.ShapeDtypeStruct(shape, jnp.bfloat16),
        jax.ShapeDtypeStruct(shape, jnp.bfloat16),
        jax.ShapeDtypeStruct(shape, jnp.float32),
        jax.ShapeDtypeStruct(shape, jnp.float32),
    ]
    if with_part:
        out_specs.append(whole_part)
        out_shape.append(jax.ShapeDtypeStruct((tokens, rows), jnp.float32))
    outs = pl.pallas_call(
        functools.partial(update_kernel, kick_scale, with_part, first),
        grid=(steps,),
        in_specs=in_specs,
        out_specs=out_specs,
        out_shape=out_shape,
        input_output_aliases=aliases,
        compiler_params=pltpu.CompilerParams(vmem_limit_bytes=VMEM_LIMIT),
        cost_estimate=pl.CostEstimate(
            flops=(8 if with_part else 4) * tokens * rows * width,
            bytes_accessed=(8 * tokens + 28 * rows) * width,
            transcendentals=0,
        ),
        name="update_step",
    )(*operands)
    return (outs[4] if with_part else None), tuple(outs[:4])


def saved_kernel(kick_scale, size, table, *refs):
    gate_pieces = refs[: 2 * size - 1]
    up_pieces = refs[2 * size - 1 : 4 * size - 2]
    grads, weight, momentum, noise = refs[4 * size - 2 : 4 * size + 2]
    new_down, next_down, gate_factor, up_factor, hidden = refs[-5:]
    rows = gate_pieces[0].shape[0]

    def piece(pieces, at):
        if at == 0:
            return pieces[0][...].astype(jnp.float32)
        one, other = pieces[2 * at - 1], pieces[2 * at]
        return jnp.where(
            table[at] == 1, one[...].astype(jnp.float32), other[...].astype(jnp.float32)
        )

    for part in range(size):
        gate_wide = piece(gate_pieces, part)
        up_wide = piece(up_pieces, part)
        sigmoid_gate = 0.5 + 0.5 * jnp.tanh(0.5 * gate_wide)
        silu_gate = gate_wide * sigmoid_gate
        slope = sigmoid_gate * (1.0 + gate_wide * (1.0 - sigmoid_gate))
        at = pl.ds(pl.multiple_of(table[size + part] * rows, rows), rows)
        gate_factor[at, :] = (up_wide * slope).astype(jnp.bfloat16)
        up_factor[at, :] = silu_gate.astype(jnp.bfloat16)
        hidden[at, :] = (silu_gate * up_wide).astype(jnp.bfloat16)
    wgrad = contract(hidden[...], grads[...], 0, 0)
    moved, fresh = moved_and_fresh(weight[...], momentum[...], wgrad, noise[...], kick_scale)
    next_down[...] = moved
    new_down[...] = fresh


def saved_step(
    kick_scale, start, stop, table, gate_pieces, up_pieces, grads, weight, momentum, noise, made
):
    size = table.shape[0] // 2
    rows = gate_pieces[0][0].shape[0]
    tokens, columns = grads.shape
    width = stop - start
    tile = tile_of(width)
    first = start // tile
    pieces = [*gate_pieces, *up_pieces]
    piece_specs = [pl.BlockSpec((rows, tile), lambda j, at=at: (at, first + j)) for _, at in pieces]
    block = pl.BlockSpec((tile, columns), lambda j: (first + j, 0))
    whole = pl.BlockSpec((tokens, columns), lambda j: (0, 0))
    factor = pl.BlockSpec((tokens, tile), lambda j: (0, j))
    operands = [table, *[array for array, _ in pieces], grads, weight, momentum, noise]
    in_specs = [pl.BlockSpec(memory_space=pltpu.SMEM), *piece_specs, whole] + [block] * 3
    aliases = {}
    if made is not None:
        aliases = {len(operands) + i: i for i in range(2)}
        in_specs += [pl.BlockSpec(memory_space=pl.ANY)] * 2
        operands += made
    outs = pl.pallas_call(
        functools.partial(saved_kernel, kick_scale, size),
        grid=(width // tile,),
        in_specs=in_specs,
        out_specs=[block, block, factor, factor],
        out_shape=[
            jax.ShapeDtypeStruct(weight.shape, jnp.bfloat16),
            jax.ShapeDtypeStruct(weight.shape, jnp.float32),
            jax.ShapeDtypeStruct((tokens, width), jnp.bfloat16),
            jax.ShapeDtypeStruct((tokens, width), jnp.bfloat16),
        ],
        scratch_shapes=[pltpu.VMEM((tokens, tile), jnp.bfloat16)],
        input_output_aliases=aliases,
        compiler_params=pltpu.CompilerParams(vmem_limit_bytes=VMEM_LIMIT),
        cost_estimate=pl.CostEstimate(
            flops=2 * tokens * width * columns,
            bytes_accessed=12 * tokens * width + 14 * width * columns,
            transcendentals=tokens * width,
        ),
        name="saved_step",
    )(*operands)
    return tuple(outs[:2]), tuple(outs[2:])


def relay_step(behind, ahead, axis, step):
    size = lax.axis_size(axis)
    up = [(i, i + 1) for i in range(step - 1, size - 1)]
    down = [(i, i - 1) for i in range(1, size - step + 1)]
    return lax.ppermute(behind, axis, up), lax.ppermute(ahead, axis, down)


def relayed(arrays, axis):
    size = lax.axis_size(axis)
    me = lax.axis_index(axis).astype(jnp.int32)
    pieces = []
    for own in arrays:
        behind, ahead = [own], [own]
        for step in range(1, size):
            from_back, from_front = relay_step(behind[-1], ahead[-1], axis, step)
            behind.append(from_back)
            ahead.append(from_front)
        pieces.append([(own, 0)])
        for back in range(1, size):
            pieces[-1] += [(behind[back], 0), (ahead[size - back], 0)]
    backs = jnp.arange(size, dtype=jnp.int32)
    table = jnp.concatenate([(me >= backs).astype(jnp.int32), (me - backs + size) % size])
    return pieces, table


OUTWARD = ((1, 0), (2, 3))
INWARD = ((0, 1), (3, 2))
MIDDLE = ((1, 2), (2, 1))


def relayed_by_four(arrays, terms, axis, early):
    me = lax.axis_index(axis).astype(jnp.int32)
    gate, up = arrays
    gate_b1, gate_a1 = relay_step(gate, gate, axis, 1)
    up_b1, up_a1 = relay_step(up, up, axis, 1)
    gate_b2, gate_a2 = relay_step(gate_b1, gate_a1, axis, 2)
    up_b2, up_a2 = relay_step(up_b1, up_a1, axis, 2)
    gate_out3 = lax.ppermute(jnp.where(me == 1, gate_a2, gate_b2), axis, OUTWARD)
    up_out3 = lax.ppermute(jnp.where(me == 1, up_a2, up_b2), axis, OUTWARD)
    terms, ins = list(lax.optimization_barrier((*terms, early))[:-1]), []
    for at in range(len(terms)):
        terms[at] = after(terms[at], ins[min(at, 3) - 1] if at else gate_b1)
        ins.append(lax.ppermute(terms[at], axis, INWARD))
    inner, mids = [], []
    sums = []

    def send_inner(at, *ties):
        inner.append(add_wide(terms[at], ins[at], ties))
        mids.append(lax.ppermute(inner[at], axis, MIDDLE))

    def send_total(at, *ties):
        sums.append(outward_sum(add_wide(inner[at], mids[at], ties), axis))

    send_inner(0, up_a2, up_b2)
    send_inner(1, gate_out3)
    send_total(0, gate_out3)
    send_inner(2, sums[0][1])
    send_total(1, up_out3)
    send_inner(3, sums[1][1])
    send_inner(4, mids[2])
    pieces = [
        [(gate, 0), (gate_a1, 0), (gate_b1, 0), (gate_a2, 0), (gate_b2, 0)],
        [(up, 0), (up_a1, 0), (up_b1, 0), (up_a2, 0), (up_b2, 0)],
    ]
    pieces[0] += [(gate_out3, 0), (gate_b1, 0)]
    pieces[1] += [(up_out3, 0), (up_b1, 0)]
    end = (me == 0) | (me == 3)
    flags = [me < 3, me < 3, me < 2, end]
    places = [me, jnp.where(me < 3, me + 1, 2), (me + 2) % 4, jnp.where(end, 3 - me, me - 1)]
    table = jnp.stack([flag.astype(jnp.int32) for flag in flags] + places)
    return pieces, table, sums, send_total


def inward_sum(term, axis, ties):
    size = lax.axis_size(axis)
    held = term
    for step in range(size // 2 - 1):
        pairs = [(step, step + 1), (size - 1 - step, size - 2 - step)]
        held = add_wide(held, lax.ppermute(held, axis, pairs), ties if step == 0 else ())
    return held


def middle_sum(held, axis, ties):
    half = lax.axis_size(axis) // 2
    across = lax.ppermute(held, axis, [(half - 1, half), (half, half - 1)])
    return add_wide(held, across, ties), across


def outward_sum(held, axis):
    size = lax.axis_size(axis)
    index = lax.axis_index(axis)
    half = size // 2
    received, flag = held, jnp.zeros((1,), jnp.int32)
    for step in range(half - 1):
        if step:
            held = jnp.where(flag[0] == 1, received, held)
        pairs = [(half - 1 - step, half - 2 - step), (half + step, half + 1 + step)]
        received = lax.ppermute(held, axis, pairs)
        arrived = (index == half - 2 - step) | (index == half + 1 + step)
        flag = arrived.astype(jnp.int32).reshape((1,))
    return received, held, flag


def row_sums(terms, axis):
    sums = []
    for term in terms:
        if lax.axis_size(axis) % 2:
            total = lax.psum(term, axis)
            sums.append((total, total, jnp.zeros((1,), jnp.int32)))
        else:
            held, _ = middle_sum(inward_sum(term, axis, ()), axis, ())
            sums.append(outward_sum(held, axis))
    return sums


def parts_sum(parts, axis):
    if len(parts) == 1:
        return lax.psum_scatter(parts[0], axis, scatter_dimension=0, tiled=True)
    return add_wide(parts[0], lax.ppermute(parts[1], axis, [(0, 1), (1, 0)]))


def shards(
    section_inputs,
    out_grad,
    saved_gate,
    saved_up,
    gate_weight,
    up_weight,
    down_weight,
    momentum_gate,
    momentum_up,
    momentum_down,
    noise_gate,
    noise_up,
    noise_down,
):
    size = lax.axis_size("row")
    saved = (saved_gate[0], saved_up[0])
    grads_full = lax.all_gather(out_grad[0], "col", axis=0, tiled=True)
    inputs_full = lax.all_gather(section_inputs[0], "col", axis=0, tiled=True)
    inputs_t = inputs_full.T
    tokens = inputs_full.shape[0]
    kick_scale = float(tokens) ** (-0.5)
    down_local = down_weight[0]
    unit = down_local.shape[0] // sum(CHUNKS)
    starts = [unit * sum(CHUNKS[:at]) for at in range(len(CHUNKS))]
    stops = starts[1:] + [down_local.shape[0]]
    terms = [
        contract(grads_full, down_local[start:stop], 1, 1).astype(jnp.bfloat16)
        for start, stop in zip(starts, stops)
    ]
    send_total = None
    if size == 4:
        pieces, table, sums, send_total = relayed_by_four(saved, terms, "row", inputs_t)
    else:
        pieces, table = relayed(saved, "row")
        sums = row_sums(terms, "row")

    middle = starts[2]
    factored, downs = [], None
    for start, stop in ((0, middle), (middle, stops[-1])):
        if start and sums:
            table = after(table, sums[1][1])
        downs, factors = saved_step(
            kick_scale,
            start,
            stop,
            table,
            *pieces,
            grads_full,
            down_local,
            momentum_down[0],
            noise_down[0],
            downs,
        )
        factored.append((start, factors))
    new_down, next_down = downs
    weights = (gate_weight[0], up_weight[0])
    arrays = weights + (momentum_gate[0], momentum_up[0], noise_gate[0], noise_up[0])
    if send_total is not None:
        send_total(2, factored[1][1][0])
    part, made = None, None
    for at, start in enumerate(starts[:-1]):
        part, made = update_step(
            kick_scale, start, sums[at], factored[at > 1], inputs_t, arrays, part, made, True
        )
        if at == 0 and send_total is not None:
            send_total(3, part)
            send_total(4, sums[3][1])
    parts = part_step(starts[-1], sums[-1], factored[1], weights, part, "col")
    _, made = update_step(
        kick_scale, starts[-1], sums[-1], factored[1], inputs_t, arrays, None, made, False
    )
    new_gate, new_up, next_gate, next_up = made
    input_grad = parts_sum(parts, "col")
    passed = from_behind(input_grad, "section", -1)
    return tuple(
        value[None]
        for value in (passed, new_gate, new_up, new_down, next_gate, next_up, next_down)
    )


def solution(mesh):
    in_specs = (
        P("section", "col", "row"),
        P("section", "col", "row"),
        P("section", "row", "col"),
        P("section", "row", "col"),
        P("section", "row", "col"),
        P("section", "row", "col"),
        P("section", "col", "row"),
        P("section", "row", "col"),
        P("section", "row", "col"),
        P("section", "col", "row"),
        P("section", "row", "col"),
        P("section", "row", "col"),
        P("section", "col", "row"),
    )
    out_specs = (
        P("section", "col", "row"),
        P("section", "row", "col"),
        P("section", "row", "col"),
        P("section", "col", "row"),
        P("section", "row", "col"),
        P("section", "row", "col"),
        P("section", "col", "row"),
    )
    return jax.shard_map(shards, mesh=mesh, in_specs=in_specs, out_specs=out_specs, check_vma=False)
```

```python
import functools

import jax
import jax.numpy as jnp
from jax import lax
from jax.experimental import pallas as pl
from jax.experimental.pallas import tpu as pltpu
from jax.sharding import PartitionSpec as P

FRICTION = 0.1
DRIFT = 0.01
CHUNKS = (2, 2, 2, 1, 1)
VMEM_LIMIT = 56 * 1024 * 1024


def from_behind(shard, axis, by):
    size = lax.axis_size(axis)
    pairs = [(i, i + by) for i in range(size) if 0 <= i + by < size]
    return lax.ppermute(shard, axis, pairs)


def contract(left, right, left_dim, right_dim):
    return lax.dot_general(
        left, right, (((left_dim,), (right_dim,)), ((), ())), preferred_element_type=jnp.float32
    )


def moved_and_fresh(weight, momentum, gradient, noise, kick_scale):
    moved = (
        (1.0 - FRICTION) * momentum
        - kick_scale * gradient
        + (2.0 * FRICTION) ** 0.5 * noise.astype(jnp.float32)
    )
    fresh = (weight.astype(jnp.float32) + DRIFT * moved).astype(jnp.bfloat16)
    return moved, fresh


def after(value, *ties):
    return lax.optimization_barrier((value, *ties))[0]


def add_wide(left, right, ties=()):
    right = after(right, *ties) if ties else right
    return (left.astype(jnp.float32) + right.astype(jnp.float32)).astype(jnp.bfloat16)


def tile_of(width, largest=512):
    for tile in (largest, 256, 128):
        if width % tile == 0:
            return tile
    return width


def pre_grads(flag, received, held, gate_factor, up_factor):
    hidden_grad = jnp.where(
        flag[0] == 1, received[...].astype(jnp.float32), held[...].astype(jnp.float32)
    )
    gate_grad = (hidden_grad * gate_factor[...].astype(jnp.float32)).astype(jnp.bfloat16)
    up_grad = (hidden_grad * up_factor[...].astype(jnp.float32)).astype(jnp.bfloat16)
    return gate_grad, up_grad


def update_kernel(
    kick_scale,
    with_part,
    first,
    flag,
    received,
    held,
    gate_factor,
    up_factor,
    inputs_t,
    gate_weight,
    up_weight,
    momentum_gate,
    momentum_up,
    noise_gate,
    noise_up,
    *rest,
):
    if with_part:
        part = rest[-1]
        rest = rest[:-1]

        @pl.when(pl.program_id(0) == 0)
        def _():
            part[...] = jnp.zeros_like(part) if first else rest[0][...]

    new_gate, new_up, next_gate, next_up = rest[-4:]
    gate_grad, up_grad = pre_grads(flag, received, held, gate_factor, up_factor)
    gate_here = gate_weight[...]
    up_here = up_weight[...]
    if with_part:
        part[...] += contract(gate_grad, gate_here, 1, 1) + contract(up_grad, up_here, 1, 1)
    gate_wgrad = contract(inputs_t[...], gate_grad, 1, 0)
    moved, fresh = moved_and_fresh(
        gate_here, momentum_gate[...], gate_wgrad, noise_gate[...], kick_scale
    )
    next_gate[...] = moved
    new_gate[...] = fresh
    up_wgrad = contract(inputs_t[...], up_grad, 1, 0)
    moved, fresh = moved_and_fresh(up_here, momentum_up[...], up_wgrad, noise_up[...], kick_scale)
    next_up[...] = moved
    new_up[...] = fresh


def chunk_specs(start, base, tokens, rows, width, tile):
    steps = width // tile
    at = start // tile
    there_at = (start - base) // tile
    here = pl.BlockSpec((tokens, tile), lambda j: (0, j))
    there = pl.BlockSpec((tokens, tile), lambda j: (0, there_at + j))
    block = pl.BlockSpec((rows, tile), lambda j: (0, at + j))
    flag = pl.BlockSpec(memory_space=pltpu.SMEM)
    return steps, block, [flag, here, here, there, there]


def part_kernel(
    halves, col, flag, received, held, gate_factor, up_factor, gate_weight, up_weight, before, *rest
):
    outs, part = rest[:-1], rest[-1]

    @pl.when(pl.program_id(0) == 0)
    def _():
        part[...] = before[...]

    gate_grad, up_grad = pre_grads(flag, received, held, gate_factor, up_factor)
    part[...] += contract(gate_grad, gate_weight[...], 1, 1) + contract(
        up_grad, up_weight[...], 1, 1
    )

    @pl.when(pl.program_id(0) == pl.num_programs(0) - 1)
    def _():
        if not halves:
            outs[0][...] = part[...].astype(jnp.bfloat16)
            return
        half = part.shape[0] // 2
        for out, which in ((outs[0], col[0]), (outs[1], 1 - col[0])):
            at = pl.ds(pl.multiple_of(which * half, half), half)
            out[...] = part[at, :].astype(jnp.bfloat16)


def part_step(start, hidden, factored, weights, part, axis):
    received, held, flag = hidden
    base, factors = factored
    tokens, width = held.shape
    rows = weights[0].shape[0]
    halves = lax.axis_size(axis) == 2
    tile = tile_of(width)
    steps, block, in_specs = chunk_specs(start, base, tokens, rows, width, tile)
    whole = pl.BlockSpec((tokens, rows), lambda j: (0, 0))
    half = pl.BlockSpec((tokens // 2, rows), lambda j: (0, 0))
    index = lax.axis_index(axis).astype(jnp.int32).reshape((1,))
    return pl.pallas_call(
        functools.partial(part_kernel, halves),
        grid=(steps,),
        in_specs=[pl.BlockSpec(memory_space=pltpu.SMEM)] + in_specs + [block] * 2 + [whole],
        out_specs=[half] * 2 if halves else [whole],
        out_shape=[jax.ShapeDtypeStruct((tokens // 2, rows), jnp.bfloat16)] * 2
        if halves
        else [jax.ShapeDtypeStruct((tokens, rows), jnp.bfloat16)],
        scratch_shapes=[pltpu.VMEM((tokens, rows), jnp.float32)],
        compiler_params=pltpu.CompilerParams(vmem_limit_bytes=VMEM_LIMIT),
        cost_estimate=pl.CostEstimate(
            flops=4 * tokens * rows * width,
            bytes_accessed=(8 * tokens + 4 * rows) * width + 6 * tokens * rows,
            transcendentals=0,
        ),
        name="part_step",
    )(index, flag, received, held, *factors, *weights, part)


def update_step(kick_scale, start, hidden, factored, inputs_t, arrays, part, made, with_part):
    received, held, flag = hidden
    base, factors = factored
    tokens, width = held.shape
    rows, columns = arrays[0].shape
    tile = tile_of(width, 512 if with_part else 256)
    first = part is None
    steps, block, in_specs = chunk_specs(start, base, tokens, rows, width, tile)
    whole_inputs = pl.BlockSpec((rows, tokens), lambda j: (0, 0))
    whole_part = pl.BlockSpec((tokens, rows), lambda j: (0, 0))
    in_specs += [whole_inputs] + [block] * 6
    operands = [flag, received, held, *factors, inputs_t, *arrays]
    if with_part and not first:
        in_specs.append(whole_part)
        operands.append(part)
    aliases = {}
    if made is not None:
        aliases = {len(operands) + i: i for i in range(4)}
        in_specs += [pl.BlockSpec(memory_space=pl.ANY)] * 4
        operands += made
    shape = (rows, columns)
    out_specs = [block] * 4
    out_shape = [
        jax.ShapeDtypeStruct(shape, jnp.bfloat16),
        jax.ShapeDtypeStruct(shape, jnp.bfloat16),
        jax.ShapeDtypeStruct(shape, jnp.float32),
        jax.ShapeDtypeStruct(shape, jnp.float32),
    ]
    if with_part:
        out_specs.append(whole_part)
        out_shape.append(jax.ShapeDtypeStruct((tokens, rows), jnp.float32))
    outs = pl.pallas_call(
        functools.partial(update_kernel, kick_scale, with_part, first),
        grid=(steps,),
        in_specs=in_specs,
        out_specs=out_specs,
        out_shape=out_shape,
        input_output_aliases=aliases,
        compiler_params=pltpu.CompilerParams(vmem_limit_bytes=VMEM_LIMIT),
        cost_estimate=pl.CostEstimate(
            flops=(8 if with_part else 4) * tokens * rows * width,
            bytes_accessed=(8 * tokens + 28 * rows) * width,
            transcendentals=0,
        ),
        name="update_step",
    )(*operands)
    return (outs[4] if with_part else None), tuple(outs[:4])


def saved_kernel(kick_scale, size, table, *refs):
    gate_pieces = refs[: 2 * size - 1]
    up_pieces = refs[2 * size - 1 : 4 * size - 2]
    grads, weight, momentum, noise = refs[4 * size - 2 : 4 * size + 2]
    new_down, next_down, gate_factor, up_factor, hidden = refs[-5:]
    rows = gate_pieces[0].shape[0]

    def piece(pieces, at, flags):
        if at == 0:
            return pieces[0][...].astype(jnp.float32)
        one, other = pieces[2 * at - 1], pieces[2 * at]
        return jnp.where(
            table[flags + at] == 1, one[...].astype(jnp.float32), other[...].astype(jnp.float32)
        )

    for part in range(size):
        gate_wide = piece(gate_pieces, part, 0)
        up_wide = piece(up_pieces, part, size)
        sigmoid_gate = 0.5 + 0.5 * jnp.tanh(0.5 * gate_wide)
        silu_gate = gate_wide * sigmoid_gate
        slope = sigmoid_gate * (1.0 + gate_wide * (1.0 - sigmoid_gate))
        at = pl.ds(pl.multiple_of(table[2 * size + part] * rows, rows), rows)
        gate_factor[at, :] = (up_wide * slope).astype(jnp.bfloat16)
        up_factor[at, :] = silu_gate.astype(jnp.bfloat16)
        hidden[at, :] = (silu_gate * up_wide).astype(jnp.bfloat16)
    wgrad = contract(hidden[...], grads[...], 0, 0)
    moved, fresh = moved_and_fresh(weight[...], momentum[...], wgrad, noise[...], kick_scale)
    next_down[...] = moved
    new_down[...] = fresh


def saved_step(
    kick_scale, start, stop, table, gate_pieces, up_pieces, grads, weight, momentum, noise, made
):
    size = table.shape[0] // 3
    rows = gate_pieces[0][0].shape[0]
    tokens, columns = grads.shape
    width = stop - start
    tile = tile_of(width)
    first = start // tile
    pieces = [*gate_pieces, *up_pieces]
    piece_specs = [pl.BlockSpec((rows, tile), lambda j, at=at: (at, first + j)) for _, at in pieces]
    block = pl.BlockSpec((tile, columns), lambda j: (first + j, 0))
    whole = pl.BlockSpec((tokens, columns), lambda j: (0, 0))
    factor = pl.BlockSpec((tokens, tile), lambda j: (0, j))
    operands = [table, *[array for array, _ in pieces], grads, weight, momentum, noise]
    in_specs = [pl.BlockSpec(memory_space=pltpu.SMEM), *piece_specs, whole] + [block] * 3
    aliases = {}
    if made is not None:
        aliases = {len(operands) + i: i for i in range(2)}
        in_specs += [pl.BlockSpec(memory_space=pl.ANY)] * 2
        operands += made
    outs = pl.pallas_call(
        functools.partial(saved_kernel, kick_scale, size),
        grid=(width // tile,),
        in_specs=in_specs,
        out_specs=[block, block, factor, factor],
        out_shape=[
            jax.ShapeDtypeStruct(weight.shape, jnp.bfloat16),
            jax.ShapeDtypeStruct(weight.shape, jnp.float32),
            jax.ShapeDtypeStruct((tokens, width), jnp.bfloat16),
            jax.ShapeDtypeStruct((tokens, width), jnp.bfloat16),
        ],
        scratch_shapes=[pltpu.VMEM((tokens, tile), jnp.bfloat16)],
        input_output_aliases=aliases,
        compiler_params=pltpu.CompilerParams(vmem_limit_bytes=VMEM_LIMIT),
        cost_estimate=pl.CostEstimate(
            flops=2 * tokens * width * columns,
            bytes_accessed=12 * tokens * width + 14 * width * columns,
            transcendentals=tokens * width,
        ),
        name="saved_step",
    )(*operands)
    return tuple(outs[:2]), tuple(outs[2:])


def relay_step(behind, ahead, axis, step):
    size = lax.axis_size(axis)
    up = [(i, i + 1) for i in range(step - 1, size - 1)]
    down = [(i, i - 1) for i in range(1, size - step + 1)]
    return lax.ppermute(behind, axis, up), lax.ppermute(ahead, axis, down)


def relayed(arrays, axis):
    size = lax.axis_size(axis)
    me = lax.axis_index(axis).astype(jnp.int32)
    pieces = []
    for own in arrays:
        behind, ahead = [own], [own]
        for step in range(1, size):
            from_back, from_front = relay_step(behind[-1], ahead[-1], axis, step)
            behind.append(from_back)
            ahead.append(from_front)
        pieces.append([(own, 0)])
        for back in range(1, size):
            pieces[-1] += [(behind[back], 0), (ahead[size - back], 0)]
    backs = jnp.arange(size, dtype=jnp.int32)
    flags = (me >= backs).astype(jnp.int32)
    table = jnp.concatenate([flags, flags, (me - backs + size) % size])
    return pieces, table


OUTWARD = ((1, 0), (2, 3))
INWARD = ((0, 1), (3, 2))
MIDDLE = ((1, 2), (2, 1))


def relayed_by_four(arrays, terms, axis, early):
    me = lax.axis_index(axis).astype(jnp.int32)
    gate, up = arrays
    gate_out1 = lax.ppermute(gate, axis, OUTWARD)
    gate_b1 = lax.ppermute(gate, axis, [(0, 1), (1, 2)])
    gate_a1 = after(lax.ppermute(gate, axis, [(2, 1), (3, 2)]), gate_out1)
    up_b1, up_a1 = relay_step(up, up, axis, 1)
    gate_b2, gate_a2 = relay_step(gate_b1, gate_a1, axis, 2)
    up_b2, up_a2 = relay_step(up_b1, up_a1, axis, 2)
    gate_out3 = lax.ppermute(jnp.where(me == 1, gate_a2, gate_b2), axis, OUTWARD)
    up_out3 = lax.ppermute(jnp.where(me == 1, up_a2, up_b2), axis, OUTWARD)
    terms, ins = list(lax.optimization_barrier((*terms, early))[:-1]), []
    for at in range(len(terms)):
        terms[at] = after(terms[at], ins[min(at, 3) - 1] if at else gate_b1)
        ins.append(lax.ppermute(terms[at], axis, INWARD))
    inner, mids = [], []
    sums = []

    def send_inner(at, *ties):
        inner.append(add_wide(terms[at], ins[at], ties))
        mids.append(lax.ppermute(inner[at], axis, MIDDLE))

    def send_total(at, *ties):
        sums.append(outward_sum(add_wide(inner[at], mids[at], ties), axis))

    send_inner(0, up_a2, up_b2)
    send_inner(1, gate_out3)
    send_total(0, gate_out3)
    send_inner(2, sums[0][1])
    send_total(1, up_out3)
    send_inner(3, sums[1][1])
    send_inner(4, mids[2])
    pieces = [
        [gate, gate_a1, gate_out1, gate_a2, gate_b2, gate_out3, gate_b1],
        [up, up_a1, up_b1, up_a2, up_b2, up_out3, up_b1],
    ]
    pieces = [[(array, 0) for array in group] for group in pieces]
    end = (me == 0) | (me == 3)
    flags = [end, ~end, me < 2, end] + [end, me < 3, me < 2, end]
    places = [me, jnp.where(me < 3, me + 1, 2), (me + 2) % 4, jnp.where(end, 3 - me, me - 1)]
    table = jnp.stack([flag.astype(jnp.int32) for flag in flags] + places)
    return pieces, table, sums, send_total


def inward_sum(term, axis, ties):
    size = lax.axis_size(axis)
    held = term
    for step in range(size // 2 - 1):
        pairs = [(step, step + 1), (size - 1 - step, size - 2 - step)]
        held = add_wide(held, lax.ppermute(held, axis, pairs), ties if step == 0 else ())
    return held


def middle_sum(held, axis, ties):
    half = lax.axis_size(axis) // 2
    across = lax.ppermute(held, axis, [(half - 1, half), (half, half - 1)])
    return add_wide(held, across, ties), across


def outward_sum(held, axis):
    size = lax.axis_size(axis)
    index = lax.axis_index(axis)
    half = size // 2
    received, flag = held, jnp.zeros((1,), jnp.int32)
    for step in range(half - 1):
        if step:
            held = jnp.where(flag[0] == 1, received, held)
        pairs = [(half - 1 - step, half - 2 - step), (half + step, half + 1 + step)]
        received = lax.ppermute(held, axis, pairs)
        arrived = (index == half - 2 - step) | (index == half + 1 + step)
        flag = arrived.astype(jnp.int32).reshape((1,))
    return received, held, flag


def row_sums(terms, axis):
    sums = []
    for term in terms:
        if lax.axis_size(axis) % 2:
            total = lax.psum(term, axis)
            sums.append((total, total, jnp.zeros((1,), jnp.int32)))
        else:
            held, _ = middle_sum(inward_sum(term, axis, ()), axis, ())
            sums.append(outward_sum(held, axis))
    return sums


def parts_sum(parts, axis):
    if len(parts) == 1:
        return lax.psum_scatter(parts[0], axis, scatter_dimension=0, tiled=True)
    return add_wide(parts[0], lax.ppermute(parts[1], axis, [(0, 1), (1, 0)]))


def shards(
    section_inputs,
    out_grad,
    saved_gate,
    saved_up,
    gate_weight,
    up_weight,
    down_weight,
    momentum_gate,
    momentum_up,
    momentum_down,
    noise_gate,
    noise_up,
    noise_down,
):
    size = lax.axis_size("row")
    saved = (saved_gate[0], saved_up[0])
    grads_full = lax.all_gather(out_grad[0], "col", axis=0, tiled=True)
    inputs_full = lax.all_gather(section_inputs[0], "col", axis=0, tiled=True)
    inputs_t = inputs_full.T
    tokens = inputs_full.shape[0]
    kick_scale = float(tokens) ** (-0.5)
    down_local = down_weight[0]
    unit = down_local.shape[0] // sum(CHUNKS)
    starts = [unit * sum(CHUNKS[:at]) for at in range(len(CHUNKS))]
    stops = starts[1:] + [down_local.shape[0]]
    terms = [
        contract(grads_full, down_local[start:stop], 1, 1).astype(jnp.bfloat16)
        for start, stop in zip(starts, stops)
    ]
    send_total = None
    if size == 4:
        pieces, table, sums, send_total = relayed_by_four(saved, terms, "row", inputs_t)
    else:
        pieces, table = relayed(saved, "row")
        sums = row_sums(terms, "row")

    middle = starts[2]
    factored, downs = [], None
    for start, stop in ((0, middle), (middle, stops[-1])):
        if start and sums:
            table = after(table, sums[1][1])
        downs, factors = saved_step(
            kick_scale,
            start,
            stop,
            table,
            *pieces,
            grads_full,
            down_local,
            momentum_down[0],
            noise_down[0],
            downs,
        )
        factored.append((start, factors))
    new_down, next_down = downs
    weights = (gate_weight[0], up_weight[0])
    arrays = weights + (momentum_gate[0], momentum_up[0], noise_gate[0], noise_up[0])
    if send_total is not None:
        send_total(2, factored[1][1][0])
    part, made = None, None
    for at, start in enumerate(starts[:-1]):
        part, made = update_step(
            kick_scale, start, sums[at], factored[at > 1], inputs_t, arrays, part, made, True
        )
        if at == 0 and send_total is not None:
            send_total(3, part)
            send_total(4, sums[3][1])
    parts = part_step(starts[-1], sums[-1], factored[1], weights, part, "col")
    _, made = update_step(
        kick_scale, starts[-1], sums[-1], factored[1], inputs_t, arrays, None, made, False
    )
    new_gate, new_up, next_gate, next_up = made
    input_grad = parts_sum(parts, "col")
    passed = from_behind(input_grad, "section", -1)
    return tuple(
        value[None]
        for value in (passed, new_gate, new_up, new_down, next_gate, next_up, next_down)
    )


def solution(mesh):
    in_specs = (
        P("section", "col", "row"),
        P("section", "col", "row"),
        P("section", "row", "col"),
        P("section", "row", "col"),
        P("section", "row", "col"),
        P("section", "row", "col"),
        P("section", "col", "row"),
        P("section", "row", "col"),
        P("section", "row", "col"),
        P("section", "col", "row"),
        P("section", "row", "col"),
        P("section", "row", "col"),
        P("section", "col", "row"),
    )
    out_specs = (
        P("section", "col", "row"),
        P("section", "row", "col"),
        P("section", "row", "col"),
        P("section", "col", "row"),
        P("section", "row", "col"),
        P("section", "row", "col"),
        P("section", "col", "row"),
    )
    return jax.shard_map(shards, mesh=mesh, in_specs=in_specs, out_specs=out_specs, check_vma=False)
```
